32 devices in a mesh: groups: 2 (over y), row: 4 (over z), col: 4 (over x, core).
Axes of the slice: x: 2, y: 2, z: 4, core: 2. Of those that a mesh axis runs over, the one named last changes fastest.
Arguments:
- slip: float32 [32, 16, 243], P(('groups', 'row', 'col')), parts along dimension 0, may hold values from -6 to 6
- inverse: float32 [32, 486, 243], P(('groups', 'row', 'col')), parts along dimension 0, may hold values from -0.6 to 0.6
- positions: float32 [32, 3, 81], P('groups'), parts along dimension 0
Outputs:
- updated: float32 [32, 16, 243], P(('groups', 'row', 'col')), parts along dimension 0
- residual: float32 [32, 16, 243], P(('groups', 'row', 'col')), parts along dimension 0
The draws below stay inside these ranges and needn't reach their ends.
There are 2 independent parts, one for each index of `groups`. The reference program is written for one: setup_inputs(seed, part) draws one part's arguments, and reference() takes and returns one part's arrays. A program takes and returns all parts, laid end to end along the dimension named above; each array names one. Nothing has to cross between parts.
All inputs are finite; a program needn't handle non-finite values.
Results may differ from the reference program's by a relative error of at most 0.0041.
Values may be sent and summed in bfloat16 or wider, within the bound.
No kernel may reach another device: no remote copies, remote signals or barrier semaphores. Data moves between devices by JAX's collectives and lax.ppermute only.
A program may use at most 64 MiB of HBM per device.

```python
import math
import jax
import jax.numpy as jnp
from jax import lax

BLOBS = 162
COLS = 16
HALF = 81
BLOCKS = 16
BODIES = 8


def draw_inverse(key, part):
    matrix_order = 3 * BLOBS
    narrow = 3 * HALF
    spread = 0.35 / math.sqrt(matrix_order)
    diagonal = jax.random.uniform(jax.random.fold_in(key, 12), (BLOCKS, narrow), jnp.float32, 0.2, 0.4)
    off_diag = jax.random.uniform(jax.random.fold_in(key, 11), (BLOCKS, matrix_order, narrow), jnp.float32, -spread, spread)
    row_ids = jnp.arange(matrix_order, dtype=jnp.int32)[None, :, None]
    col_ids = jnp.arange(narrow, dtype=jnp.int32)[None, None, :]
    half_ids = (jnp.arange(BLOCKS, dtype=jnp.int32) % 2)[:, None, None]
    on_diag = row_ids == half_ids * narrow + col_ids
    return off_diag + jnp.where(on_diag, diagonal[:, None, :], 0.0)


def draw_positions(key, part):
    lattice_side = int(math.ceil(BODIES ** (1.0 / 3.0)))
    if lattice_side ** 3 < BODIES:
        lattice_side = lattice_side + 1
    spacing = 8.0
    jitter = 1.0
    step_lo = 1.5
    step_hi = 2.5
    lattice_sites = jax.random.permutation(jax.random.fold_in(key, 21), lattice_side ** 3)[:BODIES]
    grid_coords = jnp.stack([lattice_sites // (lattice_side * lattice_side), lattice_sites // lattice_side % lattice_side, lattice_sites % lattice_side], axis=1).astype(jnp.float32)
    centers = grid_coords * spacing + jax.random.uniform(jax.random.fold_in(key, 22), (BODIES, 3), jnp.float32, -jitter, jitter)
    directions = jax.random.normal(jax.random.fold_in(key, 23), (BODIES, 3, BLOBS), jnp.float32)
    directions = directions / jnp.sqrt(jnp.sum(directions * directions, axis=1, keepdims=True) + 1e-06)
    step_length = jax.random.uniform(jax.random.fold_in(key, 24), (BODIES, 1, BLOBS), jnp.float32, step_lo, step_hi)
    path = jnp.cumsum(directions * step_length, axis=2)
    path = path - jnp.mean(path, axis=2, keepdims=True)
    placed = centers[:, :, None] + path
    return placed.reshape(BODIES, 3, 2, HALF).transpose(0, 2, 1, 3).reshape(BLOCKS, 3, HALF)


def block_scale(rng, dims, shards, low, high):
    def one(axis_at, parts):
        steps = jax.random.uniform(jax.random.fold_in(jax.random.fold_in(rng, 6), axis_at), (parts,), jnp.float32, low / len(shards), high / len(shards))
        return jnp.repeat(jnp.exp(steps), dims[axis_at] // parts).reshape((-1,) + (1,) * (len(dims) - axis_at - 1))

    loudness = one(*shards[0])
    for cut in shards[1:]:
        loudness = loudness * one(*cut)
    return loudness


def centred(rng, shape, scale, most, split=(), kind=jnp.bfloat16):
    factor_of = block_scale(rng, shape, split, -0.22, 0.18) if split else 1.0
    drawn = jax.random.normal(rng, shape, jnp.float32) * scale * factor_of
    return jnp.minimum(jnp.maximum(drawn, -most), most).astype(kind)


def setup_inputs(seed: int = 0, part: int = 0) -> dict:
    key_list = jax.random.split(jax.random.key(seed), 4)
    part_splits = jax.random.split(jax.random.fold_in(key_list[3], part), 4)
    return {
        "slip": centred(part_splits[0], (BLOCKS, COLS, 3 * HALF), 1.0, 6.0, ((0, 16),), jnp.float32),
        "inverse": draw_inverse(jax.random.fold_in(jax.random.fold_in(key_list[3], part), 71), part),
        "positions": draw_positions(jax.random.fold_in(jax.random.fold_in(key_list[3], part), 71), part),
    }


def rpy_tiles(left_pos, right_pos):
    separation = left_pos[:, :, :, None] - right_pos[:, :, None, :]
    dist_sq = lax.optimization_barrier(jnp.sum(separation * separation, axis=1))
    distance = jnp.sqrt(dist_sq)
    far_dist = jnp.maximum(distance, 2.0)
    near_safe = jnp.where(dist_sq > 0.0, distance, 1.0)
    far_mask = dist_sq >= 4.0
    isotropic = jnp.where(far_mask, 0.75 / far_dist * (1.0 + 2.0 / (3.0 * far_dist * far_dist)), 1.0 - 9.0 * distance / 32.0)
    anisotropic = jnp.where(far_mask, 0.75 / far_dist * (1.0 - 2.0 / (far_dist * far_dist)) / (far_dist * far_dist), 3.0 / (32.0 * near_safe))
    first_part = separation[:, :, :, None, :]
    second_part = jnp.swapaxes(separation, 1, 2)[:, None, :, :, :]
    tensor = anisotropic[:, None, :, None, :] * first_part * second_part
    identity_part = jnp.eye(3, dtype=jnp.float32)[None, :, None, :, None]
    tensor = tensor + identity_part * isotropic[:, None, :, None, :]
    tile_count = left_pos.shape[0]
    matrix_order = 3 * left_pos.shape[2]
    return tensor.reshape(tile_count, matrix_order, matrix_order).astype(jnp.bfloat16)

def join_halves(values):
    return values.reshape(BODIES, 2, COLS, 3 * HALF).transpose(0, 2, 1, 3).reshape(BODIES, COLS, 6 * HALF)

def reference(slip, inverse, positions):
    inverse_pairs = inverse.reshape(BODIES, 2, 6 * HALF, 3 * HALF)
    force = jnp.einsum('bsq,bhqp->bhsp', join_halves(slip), inverse_pairs, precision=lax.Precision.HIGHEST).reshape(BLOCKS, COLS, 3 * HALF)
    force_wire = lax.optimization_barrier(force.astype(jnp.bfloat16)).astype(jnp.float32)

    def one_row(row_index):
        left_pos = jnp.broadcast_to(positions[row_index][None], positions.shape)
        tile_blocks = rpy_tiles(left_pos, positions).astype(jnp.float32)
        return jnp.einsum('qsc,qrc->sr', force_wire, tile_blocks, precision=lax.Precision.HIGHEST)
    velocity = lax.map(one_row, jnp.arange(BLOCKS, dtype=jnp.int32))
    residual = slip - velocity
    correction = jnp.einsum('bsq,bhqp->bhsp', join_halves(residual), inverse_pairs, precision=lax.Precision.HIGHEST).reshape(BLOCKS, COLS, 3 * HALF)
    return (force + correction, residual)
```

```python
import functools

import jax
import jax.numpy as jnp
from jax import lax
from jax.experimental import pallas as pl
from jax.experimental.pallas import tpu as pltpu
from jax.sharding import PartitionSpec as P

VMEM_TILE_BYTES = 16 * 2**20


def round_up(value, step):
    return (value + step - 1) // step * step


def swapped(value):
    pairs = [(source, source ^ 1) for source in range(lax.axis_size("col"))]
    return lax.ppermute(value, "col", pairs)


class Ring:
    def __init__(self, row_count, col_count):
        self.rows, self.cols = row_count, col_count
        self.size = row_count * col_count // 2

    def place(self, row, pair):
        return pair * self.rows + jnp.where(pair % 2 == 0, row, self.rows - 1 - row)

    def body(self, place):
        pair, step = place // self.rows, place % self.rows
        row = jnp.where(pair % 2 == 0, step, self.rows - 1 - step)
        return row * (self.cols // 2) + pair

    def device(self, place, half):
        pair, step = place % self.size // self.rows, place % self.rows
        row = step if pair % 2 == 0 else self.rows - 1 - step
        return row * self.cols + 2 * pair + half

    def crossed(self, value, offset):
        pairs = []
        for place in range(self.size):
            pairs.append((self.device(place, 1), self.device(place - offset, 0)))
            pairs.append((self.device(place, 0), self.device(place + offset, 1)))
        return lax.ppermute(value, ("row", "col"), pairs)

    def offsets(self):
        steps, window = [], 1
        while window < self.size:
            steps.append(window)
            window = 3 * window
        return steps[::-1]


def pick_slots(entries, size):
    taken, picks = set(), ([], [])
    for index, offsets in enumerate(entries):
        order = (0, 1) if len(picks[0]) <= len(picks[1]) else (1, 0)
        for half in order:
            if offsets[half] % size not in taken:
                taken.add(offsets[half] % size)
                picks[half].append((index, offsets[half]))
    both = [dict(p) for p in picks]
    slots = [((i, both[0][i]), (i, both[1][i])) for i in both[0] if i in both[1]]
    lone = [[(i, both[h][i]) for i in both[h] if i not in both[1 - h]] for h in (0, 1)]
    for at in range(max(map(len, lone))):
        slots.append(tuple(lone[h][at] if at < len(lone[h]) else None for h in (0, 1)))
    return slots


def component_rows(half):
    blobs = 2 * half
    full, step = blobs // 16 * 16, round_up(blobs, 16)
    if blobs - full > 8:
        full = step
    return blobs, full, step, round_up(2 * step + full, 128)


def spread_force(force, half_index):
    columns, half = force.shape[0], force.shape[1] // 3
    blobs, full, step, width = component_rows(half)
    parts = [force[:, a * half : (a + 1) * half] for a in range(3)]
    tail = max(blobs - full, 0)

    def laid(first):
        runs = [jnp.pad(p, ((0, 0), (first, blobs - half - first))) for p in parts]
        gap = lambda n: jnp.zeros((columns, n), force.dtype)
        pieces = [runs[0]]
        if tail:
            pieces += [gap(full + 8 - blobs), runs[2][:, full:], gap(step - full - 8 - tail)]
        else:
            pieces += [gap(step - blobs)]
        pieces += [runs[1], gap(step - blobs), runs[2][:, :full]]
        row = jnp.concatenate(pieces, axis=1)
        return jnp.pad(row, ((0, 0), (0, width - row.shape[1])))

    return jnp.where(half_index == 0, laid(0), laid(half))


def rpy_rows(source, target, masks):
    apart = [s - t for s, t in zip(source, target)]
    dist_sq = apart[0] * apart[0] + apart[1] * apart[1] + apart[2] * apart[2]
    safe_sq = jnp.where(dist_sq > 0.0, dist_sq, 1.0)
    inv = lax.rsqrt(safe_sq)
    inv_sq = inv * inv
    far = dist_sq >= 4.0
    isotropic = jnp.where(far, inv * (0.75 + 0.5 * inv_sq), 1.0 - 0.28125 * (dist_sq * inv))
    anisotropic = inv * jnp.where(far, inv_sq * (0.75 - 1.5 * inv_sq), 0.09375)
    along = jnp.where(masks[0], apart[0], jnp.where(masks[1], apart[1], apart[2]))
    scaled = anisotropic * along
    third = jnp.logical_not(jnp.logical_or(masks[0], masks[1]))
    return [
        scaled * apart[b] + jnp.where(m, isotropic, 0.0)
        for b, m in enumerate((masks[0], masks[1], third))
    ]


def fill_tile(half, body, own_ref, all_ref, store):
    blobs, full, step, width = component_rows(half)
    lanes = round_up(3 * half, 128)
    source_cols = all_ref[body].T
    lane = lax.broadcasted_iota(jnp.int32, (16, lanes), 1)
    masks = (lane < half, jnp.logical_and(lane >= half, lane < 2 * half))
    for first in range(0, blobs, 16):
        source = [source_cols[first : first + 16, c : c + 1] for c in range(3)]
        for h in range(2):
            target = [own_ref[c : c + 1, h * lanes : (h + 1) * lanes] for c in range(3)]
            rows = [r.astype(jnp.bfloat16) for r in rpy_rows(source, target, masks)]
            if first < full:
                for b in range(3):
                    store(b * step + first, h, rows[b])
            else:
                mixed = jnp.concatenate([rows[0][:8], rows[2][:8]], axis=0)
                store(first, h, mixed)
                store(step + first, h, rows[1])
    used = 2 * step + full
    for first in range(used, width, 16):
        for h in range(2):
            store(first, h, jnp.zeros((16, lanes), jnp.bfloat16))


def tiles_kernel(half, slots, ids_ref, own_ref, all_ref, out_ref):
    lanes = round_up(3 * half, 128)

    def one(slot, at):
        def store(row, h, value):
            out_ref[at, row : row + 16, h * lanes : (h + 1) * lanes] = value

        fill_tile(half, ids_ref[slot], own_ref, all_ref, store)

    if slots is None:
        one(pl.program_id(0), 0)
    else:
        lax.fori_loop(0, slots, lambda s, c: (one(s, s), c)[1], 0)


def make_tiles(ids, own_pos, all_pos, half):
    slots = ids.shape[0]
    blobs, full, step, width = component_rows(half)
    shape = (slots, width, 2 * round_up(3 * half, 128))
    small = slots * shape[1] * shape[2] * 2 <= VMEM_TILE_BYTES
    whole = pl.BlockSpec(memory_space=pltpu.VMEM)
    cost = pl.CostEstimate(
        flops=slots * blobs * shape[2] * 45,
        bytes_accessed=2 * slots * shape[1] * shape[2],
        transcendentals=slots * blobs * shape[2],
    )
    params = pltpu.CompilerParams(vmem_limit_bytes=48 * 2**20)
    ids_spec = pl.BlockSpec(memory_space=pltpu.SMEM)
    if small:
        return pl.pallas_call(
            functools.partial(tiles_kernel, half, slots),
            out_shape=pltpu.VMEM(shape, jnp.bfloat16),
            in_specs=[ids_spec, whole, whole],
            out_specs=whole,
            cost_estimate=cost,
            compiler_params=params,
        )(ids, own_pos, all_pos)
    return pl.pallas_call(
        functools.partial(tiles_kernel, half, None),
        out_shape=jax.ShapeDtypeStruct(shape, jnp.bfloat16),
        grid=(slots,),
        in_specs=[ids_spec, whole, whole],
        out_specs=pl.BlockSpec((1,) + shape[1:], lambda s: (s, 0, 0)),
        cost_estimate=cost,
        compiler_params=params,
    )(ids, own_pos, all_pos)


def body_dot(first, second, inverse):
    return jnp.dot(
        jnp.concatenate([first, second], axis=-1),
        inverse,
        precision=lax.Precision.HIGHEST,
        preferred_element_type=jnp.float32,
    )


def local(slip, inverse, positions):
    ring = Ring(lax.axis_size("row"), lax.axis_size("col"))
    row, col = lax.axis_index("row"), lax.axis_index("col")
    half_index = col % 2
    own_body = row * (ring.cols // 2) + col // 2
    place = ring.place(row, col // 2)
    own_slip = slip[0]
    columns, narrow = own_slip.shape
    half = narrow // 3
    lanes = round_up(narrow, 128)

    def halves(own, other):
        return (jnp.where(half_index == 0, own, other), jnp.where(half_index == 0, other, own))

    slips = halves(own_slip, swapped(own_slip))
    force = body_dot(*slips, inverse[0])

    own_message = spread_force(force.astype(jnp.bfloat16), half_index)
    message = own_message + swapped(own_message)
    entries, values = [], []
    known, stack = [0], message[None]
    steps = ring.offsets()
    for at, step in enumerate(steps):
        got = ring.crossed(stack, step)
        entries += [(k + step, k - step) for k in known]
        values += [got[i] for i in range(len(known))]
        if at + 1 < len(steps):
            ahead, behind = halves(got, swapped(got))
            stack = jnp.concatenate([stack, ahead, behind], axis=0)
            known = known + [k + step for k in known] + [k - step for k in known]
    entries.append((0, 0))
    values.append(message)

    slots = pick_slots(entries, ring.size)
    forces, offsets = [], []
    for slot in slots:
        picked = [jnp.zeros_like(message) if s is None else values[s[0]] for s in slot]
        same = slot[0] is not None and slot[1] is not None and slot[0][0] == slot[1][0]
        forces.append(picked[0] if same else jnp.where(half_index == 0, *picked))
        offsets.append([0 if s is None else s[1] for s in slot])
    shift = jnp.where(
        half_index == 0,
        jnp.array([o[0] for o in offsets], jnp.int32),
        jnp.array([o[1] for o in offsets], jnp.int32),
    )
    ids = ring.body((place + shift + 2 * ring.size) % ring.size)

    blobs = 2 * half
    pair_pos = positions.reshape(ring.size, 2, 3, half)
    all_pos = jnp.swapaxes(pair_pos, 1, 2).reshape(ring.size, 3, blobs)
    all_pos = jnp.pad(all_pos, ((0, 0), (0, 5), (0, round_up(blobs, 128) - blobs)))
    own_pos = lax.dynamic_index_in_dim(pair_pos, own_body, 0, keepdims=False)
    own_pos = jnp.concatenate([own_pos] * 3, axis=-1)
    own_pos = jnp.pad(own_pos, ((0, 0), (0, 5), (0, lanes - narrow)))
    own_pos = jnp.concatenate([own_pos[0], own_pos[1]], axis=-1)
    tiles = make_tiles(ids, own_pos, all_pos, half)

    part = lax.dot_general(
        jnp.concatenate(forces, axis=1),
        tiles.reshape(-1, tiles.shape[2]),
        (((1,), (0,)), ((), ())),
        preferred_element_type=jnp.float32,
    )
    total = part + swapped(part)
    residuals = [s - total[:, h * lanes : h * lanes + narrow] for h, s in enumerate(slips)]
    residual = jnp.where(half_index == 0, *residuals)
    updated = force + body_dot(*residuals, inverse[0])
    return (updated[None], residual[None])


def solution(mesh):
    in_specs = (
        P(("groups", "row", "col"), None, None),
        P(("groups", "row", "col"), None, None),
        P("groups", None, None),
    )
    out_specs = (P(("groups", "row", "col"), None, None), P(("groups", "row", "col"), None, None))
    return jax.shard_map(local, mesh=mesh, in_specs=in_specs, out_specs=out_specs, check_vma=False)
```

```python
import functools

import jax
import jax.numpy as jnp
from jax import lax
from jax.experimental import pallas as pl
from jax.experimental.pallas import tpu as pltpu
from jax.sharding import PartitionSpec as P

VMEM_TILE_BYTES = 16 * 2**20
IN_VMEM = pl.BlockSpec(memory_space=pltpu.VMEM)
KERNEL_PARAMS = pltpu.CompilerParams(vmem_limit_bytes=48 * 2**20)


def work(microseconds):
    return pl.CostEstimate(flops=int(microseconds * 1.15e9), bytes_accessed=0, transcendentals=0)


def in_vmem(value):
    return pltpu.with_memory_space_constraint(value, pltpu.VMEM)


def round_up(value, step):
    return (value + step - 1) // step * step


def swapped(value):
    pairs = [(source, source ^ 1) for source in range(lax.axis_size("col"))]
    return lax.ppermute(value, "col", pairs)


class Ring:
    def __init__(self, row_count, col_count):
        self.rows, self.cols = row_count, col_count
        self.size = row_count * col_count // 2

    def place(self, row, pair):
        return pair * self.rows + jnp.where(pair % 2 == 0, row, self.rows - 1 - row)

    def body(self, place):
        pair, step = place // self.rows, place % self.rows
        row = jnp.where(pair % 2 == 0, step, self.rows - 1 - step)
        return row * (self.cols // 2) + pair

    def device(self, place, half):
        pair, step = place % self.size // self.rows, place % self.rows
        row = step if pair % 2 == 0 else self.rows - 1 - step
        return row * self.cols + 2 * pair + half

    def crossed(self, value, offset):
        pairs = []
        for place in range(self.size):
            pairs.append((self.device(place, 1), self.device(place - offset, 0)))
            pairs.append((self.device(place, 0), self.device(place + offset, 1)))
        return lax.ppermute(value, ("row", "col"), pairs)

    def offsets(self):
        steps, window = [], 1
        while window < self.size:
            steps.append(window)
            window = 3 * window
        return steps[::-1]


def pick_slots(entries, size):
    taken, picks = set(), ([], [])
    for index, offsets in enumerate(entries):
        order = (0, 1) if len(picks[0]) <= len(picks[1]) else (1, 0)
        for half in order:
            if offsets[half] % size not in taken:
                taken.add(offsets[half] % size)
                picks[half].append((index, offsets[half]))
    both = [dict(p) for p in picks]
    slots = [((i, both[0][i]), (i, both[1][i])) for i in both[0] if i in both[1]]
    lone = [[(i, both[h][i]) for i in both[h] if i not in both[1 - h]] for h in (0, 1)]
    for at in range(max(map(len, lone))):
        slots.append(tuple(lone[h][at] if at < len(lone[h]) else None for h in (0, 1)))
    return slots


def component_rows(half):
    blobs = 2 * half
    full, step = blobs // 16 * 16, round_up(blobs, 16)
    if blobs - full > 8:
        full = step
    return blobs, full, step, round_up(2 * step + full, 128)


def spread_force(force, half_index):
    columns, half = force.shape[0], force.shape[1] // 3
    blobs, full, step, width = component_rows(half)
    parts = [force[:, a * half : (a + 1) * half] for a in range(3)]
    tail = max(blobs - full, 0)

    def laid(first):
        runs = [jnp.pad(p, ((0, 0), (first, blobs - half - first))) for p in parts]
        gap = lambda n: jnp.zeros((columns, n), force.dtype)
        pieces = [runs[0]]
        if tail:
            pieces += [gap(full + 8 - blobs), runs[2][:, full:], gap(step - full - 8 - tail)]
        else:
            pieces += [gap(step - blobs)]
        pieces += [runs[1], gap(step - blobs), runs[2][:, :full]]
        row = jnp.concatenate(pieces, axis=1)
        return jnp.pad(row, ((0, 0), (0, width - row.shape[1])))

    return jnp.where(half_index == 0, laid(0), laid(half))


def rpy_products(source, target):
    apart = [s - t for s, t in zip(source, target)]
    dist_sq = apart[0] * apart[0] + apart[1] * apart[1] + apart[2] * apart[2]
    safe_sq = jnp.where(dist_sq > 0.0, dist_sq, 1.0)
    inv = lax.rsqrt(safe_sq)
    inv_sq = inv * inv
    far = dist_sq >= 4.0
    isotropic = jnp.where(far, inv * (0.75 + 0.5 * inv_sq), 1.0 - 0.28125 * (dist_sq * inv))
    anisotropic = inv * jnp.where(far, inv_sq * (0.75 - 1.5 * inv_sq), 0.09375)
    scaled = [anisotropic * d for d in apart]
    product = {}
    for a in range(3):
        for b in range(a, 3):
            value = scaled[a] * apart[b]
            product[a, b] = product[b, a] = value + isotropic if a == b else value
    return product


def lay_lanes(pieces, half):
    pad = pieces[0].shape[1]
    lanes = round_up(3 * half, 128)
    lane = lax.broadcasted_iota(jnp.int32, (1, 128), 1)
    blocks = []
    for first in range(0, lanes, 128):
        block = None
        for a in range(3):
            low, high = a * half - first, (a + 1) * half - first
            if high <= 0 or low >= 128 or pad != 128:
                continue
            moved = pltpu.roll(pieces[a], low % 128, 1) if low % 128 else pieces[a]
            block = moved if block is None else jnp.where(lane >= low, moved, block)
        blocks.append(block)
    return blocks


def fill_tile(half, body, own_body, pos_ref, store):
    blobs, full, step, width = component_rows(half)
    pad = round_up(half, 128)
    rows = [
        jnp.concatenate([pos_ref[c, pl.ds(2 * body + h, 1), :] for h in range(2)], axis=1)
        for c in range(3)
    ]
    source_rows = jnp.concatenate(rows + [jnp.zeros((5, blobs), jnp.float32)], axis=0)
    columns = round_up(step, 128)
    source_cols = jnp.pad(source_rows, ((0, 0), (0, columns - blobs))).T
    targets = [
        [
            jnp.pad(pos_ref[c, pl.ds(2 * own_body + h, 1), :], ((0, 0), (0, pad - half)))
            for c in range(3)
        ]
        for h in range(2)
    ]
    for first in range(0, blobs, 16):
        source = [source_cols[first : first + 16, c : c + 1] for c in range(3)]
        for h in range(2):
            product = rpy_products(source, targets[h])
            laid = [lay_lanes([product[a, b] for a in range(3)], half) for b in range(3)]
            for at in range(len(laid[0])):
                block = [laid[b][at] for b in range(3)]
                if first < full:
                    for b in range(3):
                        store(b * step + first, h, at, block[b])
                else:
                    mixed = jnp.concatenate([block[0][:8], block[2][:8]], axis=0)
                    store(first, h, at, mixed)
                    store(step + first, h, at, block[1])
    used = 2 * step + full
    for first in range(used, width, 16):
        for h in range(2):
            for at in range(round_up(3 * half, 128) // 128):
                store(first, h, at, jnp.zeros((16, 128), jnp.float32))


def tile_store(out_ref, half, at):
    lanes = round_up(3 * half, 128)

    def store(row, h, block, value):
        lane = h * lanes + block * 128
        out_ref[at, row : row + 16, lane : lane + 128] = value.astype(jnp.bfloat16)

    return store


def tiles_kernel(half, ring, offsets, pos_ref, out_ref):
    row, col = lax.axis_index("row"), lax.axis_index("col")
    own_body = row * (ring.cols // 2) + col // 2
    place = ring.place(row, col // 2)
    for at, (low, high) in enumerate(offsets):
        shift = jnp.where(col % 2 == 0, low % ring.size, high % ring.size)
        body = ring.body(lax.rem(place + shift, ring.size))
        fill_tile(half, body, own_body, pos_ref, tile_store(out_ref, half, at))


def listed_tiles_kernel(half, ids_ref, pos_ref, out_ref):
    body = ids_ref[pl.program_id(0) + 1]
    fill_tile(half, body, ids_ref[0], pos_ref, tile_store(out_ref, half, 0))


def make_tiles(ring, offsets, pos, half):
    shape = (component_rows(half)[-1], 2 * round_up(3 * half, 128))
    return pl.pallas_call(
        functools.partial(tiles_kernel, half, ring, offsets),
        out_shape=pltpu.VMEM((len(offsets),) + shape, jnp.bfloat16),
        in_specs=[IN_VMEM],
        out_specs=IN_VMEM,
        cost_estimate=work(0.6 * len(offsets)),
        compiler_params=KERNEL_PARAMS,
    )(in_vmem(pos))


def make_listed_tiles(ids, pos, half):
    slots = ids.shape[0] - 1
    shape = (component_rows(half)[-1], 2 * round_up(3 * half, 128))
    return pl.pallas_call(
        functools.partial(listed_tiles_kernel, half),
        out_shape=jax.ShapeDtypeStruct((slots,) + shape, jnp.bfloat16),
        grid=(slots,),
        in_specs=[pl.BlockSpec(memory_space=pltpu.SMEM), IN_VMEM],
        out_specs=pl.BlockSpec((1,) + shape, lambda s: (s, 0, 0)),
        cost_estimate=work(0.6 * slots),
        compiler_params=KERNEL_PARAMS,
    )(ids, pos)


def split(value):
    shifted = value * 65537.0
    high = shifted - (shifted - value)
    return high.astype(jnp.bfloat16), (value - high).astype(jnp.bfloat16)


def body_product(first, second, high_ref, low_ref):
    narrow, pad = first.shape[1], high_ref.shape[0] // 2
    total = None
    for h, value in enumerate((first, second)):
        high, low = split(value)
        used = slice(h * pad, h * pad + narrow)
        both = jnp.dot(jnp.concatenate([high, low], axis=0), high_ref[used, :], preferred_element_type=jnp.float32)
        term = both[: high.shape[0]] + both[high.shape[0] :]
        term = term + jnp.dot(high, low_ref[used, :], preferred_element_type=jnp.float32)
        total = term if total is None else total + term
    return total


def force_kernel(own_ref, other_ref, high_ref, low_ref, force_ref, message_ref):
    half_index = lax.axis_index("col") % 2
    own, other = own_ref[...], other_ref[...]
    first = jnp.where(half_index == 0, own, other)
    second = jnp.where(half_index == 0, other, own)
    force = body_product(first, second, high_ref, low_ref)
    force_ref[...] = force
    message_ref[...] = spread_force(force, half_index).astype(jnp.bfloat16)


def first_forces(own, other, high, low):
    columns, narrow = own.shape
    width = component_rows(narrow // 3)[-1]
    return pl.pallas_call(
        force_kernel,
        out_shape=(
            pltpu.VMEM((columns, narrow), jnp.float32),
            pltpu.VMEM((columns, width), jnp.bfloat16),
        ),
        in_specs=[IN_VMEM] * 4,
        out_specs=(IN_VMEM,) * 2,
        cost_estimate=work(0.4),
        compiler_params=KERNEL_PARAMS,
    )(*[in_vmem(v) for v in (own, other, high, low)])


def correct_kernel(own_ref, other_ref, part_ref, other_part_ref, force_ref, high_ref, low_ref, updated_ref, residual_ref):
    half_index = lax.axis_index("col") % 2
    own, other = own_ref[...], other_ref[...]
    narrow, lanes = own.shape[1], part_ref.shape[1] // 2
    velocity = part_ref[...] + other_part_ref[...]
    first = jnp.where(half_index == 0, own, other) - velocity[:, :narrow]
    second = jnp.where(half_index == 0, other, own) - velocity[:, lanes : lanes + narrow]
    residual_ref[0] = jnp.where(half_index == 0, first, second)
    updated_ref[0] = force_ref[...] + body_product(first, second, high_ref, low_ref)


def corrected(own, other, part, other_part, force, high, low):
    columns, narrow = own.shape
    out = jax.ShapeDtypeStruct((1, columns, narrow), jnp.float32)
    return pl.pallas_call(
        correct_kernel,
        out_shape=(out, out),
        in_specs=[IN_VMEM] * 7,
        out_specs=(IN_VMEM,) * 2,
        cost_estimate=work(0.8),
        compiler_params=KERNEL_PARAMS,
    )(*[in_vmem(v) for v in (own, other, part, other_part, force, high, low)])


def stage_kernel(inverse_hbm, pos_hbm, slip_hbm, high_ref, low_ref, pos_ref, slip_ref, rows_ref, sems):
    narrow, pad = slip_hbm.shape[1], high_ref.shape[0] // 2
    halves = [pl.ds(h * narrow, narrow) for h in range(2)]
    copies = [pltpu.make_async_copy(inverse_hbm.at[r], rows_ref.at[r], sems.at[h]) for h, r in enumerate(halves)]
    copies.append(pltpu.make_async_copy(pos_hbm, pos_ref, sems.at[2]))
    copies.append(pltpu.make_async_copy(slip_hbm, slip_ref, sems.at[3]))
    for copy in copies:
        copy.start()
    for h in range(2):
        copies[h].wait()
        rows = jnp.pad(rows_ref[h * narrow : (h + 1) * narrow, 0, :], ((0, pad - narrow), (0, 0)))
        high_ref[h * pad : (h + 1) * pad, :], low_ref[h * pad : (h + 1) * pad, :] = split(rows)
    copies[2].wait()
    copies[3].wait()


def staged(inverse, pos, slip):
    narrow = slip.shape[1]
    parts = pltpu.VMEM((2 * round_up(narrow, 128), narrow), jnp.bfloat16)
    values = (inverse, pos, slip)
    return pl.pallas_call(
        stage_kernel,
        out_shape=(parts, parts) + tuple(pltpu.VMEM(v.shape, v.dtype) for v in values[1:]),
        in_specs=[pl.BlockSpec(memory_space=pltpu.HBM)] * 3,
        out_specs=(IN_VMEM,) * 4,
        scratch_shapes=[pltpu.VMEM(inverse.shape, jnp.float32), pltpu.SemaphoreType.DMA((4,))],
        cost_estimate=work(1.1),
        compiler_params=KERNEL_PARAMS,
    )(*[pltpu.with_memory_space_constraint(v, pltpu.HBM) for v in values])


def apply_kernel(picks, *refs):
    half_index = lax.axis_index("col") % 2
    out_ref, refs = refs[-1], refs[:-1]
    tiles, messages = refs[: len(picks)], refs[len(picks) :]
    used = {p[0] for pick in picks for p in pick if p is not None}
    total = None if len(messages) == max(used) + 1 else messages[-1][...]
    for tile_ref, (low, high) in zip(tiles, picks):
        blank = jnp.zeros(messages[0].shape[1:], jnp.bfloat16)
        force = [blank if p is None else messages[p[0]][p[1]] for p in (low, high)]
        taken = force[0] if low == high else jnp.where(half_index == 0, *force)
        term = jnp.dot(taken, tile_ref[0], preferred_element_type=jnp.float32)
        total = term if total is None else total + term
    out_ref[...] = total


def apply_tiles(tiles, messages, picks, start=None):
    used = sorted({p[0] for pick in picks for p in pick if p is not None})
    picks = [tuple(None if p is None else (used.index(p[0]), p[1]) for p in pick) for pick in picks]
    values = list(tiles) + [messages[i] for i in used] + ([] if start is None else [start])
    columns, lanes = messages[0].shape[1], tiles[0].shape[2]
    return pl.pallas_call(
        functools.partial(apply_kernel, picks),
        out_shape=pltpu.VMEM((columns, lanes), jnp.float32),
        in_specs=[IN_VMEM] * len(values),
        out_specs=IN_VMEM,
        cost_estimate=work(0.1 + 0.08 * len(tiles)),
        compiler_params=KERNEL_PARAMS,
    )(*[in_vmem(v) for v in values])


def local(slip, inverse, positions):
    ring = Ring(lax.axis_size("row"), lax.axis_size("col"))
    own_slip = slip[0]
    columns, narrow = own_slip.shape
    half = narrow // 3
    other_slip = swapped(own_slip)
    high, low, pos, own_slip = staged(jnp.swapaxes(inverse, 0, 1), jnp.swapaxes(positions, 0, 1), own_slip)
    force, own_message = first_forces(own_slip, other_slip, high, low)
    message = (own_message + swapped(own_message))[None]

    messages, entries = [], []
    stack, known = message, [0]
    steps = ring.offsets()
    for at, step in enumerate(steps):
        got = ring.crossed(stack, step)
        entries += [(len(messages), i, step - k) for i, k in enumerate(known)]
        messages.append(got)
        if at + 1 < len(steps):
            stack = jnp.concatenate([stack, got, swapped(got)], axis=0)
            known = known + [step - k for k in known] + [k - step for k in known]
    entries.append((len(messages), 0, 0))
    messages.append(message)

    slots = pick_slots([(e, -e) for _, _, e in entries], ring.size)
    offsets = [[0 if s is None else s[1] for s in slot] for slot in slots]
    picks = [tuple(None if s is None else entries[s[0]][:2] for s in slot) for slot in slots]

    tile_bytes = 2 * len(slots) * component_rows(half)[-1] * 2 * round_up(narrow, 128)
    if tile_bytes <= VMEM_TILE_BYTES:
        tiles = [make_tiles(ring, [o], pos, half) for o in offsets]
        last = len(steps) - 1
        early = [at for at, pick in enumerate(picks) if all(p is not None and p[0] != last for p in pick)]
        late = [at for at in range(len(picks)) if at not in early]
        part = None
        for group in (early, late):
            if group:
                part = apply_tiles([tiles[at] for at in group], messages, [picks[at] for at in group], part)
    else:
        row, col = lax.axis_index("row"), lax.axis_index("col")
        shift = jnp.where(col % 2 == 0, *[jnp.array([o[h] for o in offsets], jnp.int32) for h in (0, 1)])
        place = ring.place(row, col // 2)
        ids = ring.body((place + shift % ring.size) % ring.size)
        own_body = row * (ring.cols // 2) + col // 2
        tiles = make_listed_tiles(jnp.concatenate([own_body[None], ids]), pos, half)
        blank = jnp.zeros_like(message[0])
        forces = []
        for slot in picks:
            force_of = [blank if p is None else messages[p[0]][p[1]] for p in slot]
            forces.append(force_of[0] if slot[0] == slot[1] else jnp.where(col % 2 == 0, *force_of))
        part = jnp.dot(
            jnp.concatenate(forces, axis=1),
            tiles.reshape(-1, tiles.shape[2]),
            preferred_element_type=jnp.float32,
        )
    return corrected(own_slip, other_slip, part, swapped(part), force, high, low)


def solution(mesh):
    in_specs = (
        P(("groups", "row", "col"), None, None),
        P(("groups", "row", "col"), None, None),
        P("groups", None, None),
    )
    out_specs = (P(("groups", "row", "col"), None, None), P(("groups", "row", "col"), None, None))
    return jax.shard_map(local, mesh=mesh, in_specs=in_specs, out_specs=out_specs, check_vma=False)
```

```python
import functools

import jax
import jax.numpy as jnp
from jax import lax
from jax.experimental import pallas as pl
from jax.experimental.pallas import tpu as pltpu
from jax.sharding import PartitionSpec as P

VMEM_TILE_BYTES = 16 * 2**20
TILE_TIME = 0.6
LITTLE = 0.01
IN_VMEM = pl.BlockSpec(memory_space=pltpu.VMEM)
KERNEL_PARAMS = pltpu.CompilerParams(vmem_limit_bytes=48 * 2**20)


def work(microseconds):
    return pl.CostEstimate(flops=int(microseconds * 1.15e9), bytes_accessed=0, transcendentals=0)


def in_vmem(value):
    return pltpu.with_memory_space_constraint(value, pltpu.VMEM)


def round_up(value, step):
    return (value + step - 1) // step * step


def swapped(value):
    pairs = [(source, source ^ 1) for source in range(lax.axis_size("col"))]
    return lax.ppermute(value, "col", pairs)


class Grid:
    def __init__(self, row_count, col_count):
        self.rows, self.pairs = row_count, col_count // 2

    def moved(self, value, steps):
        links = []
        for row in range(self.rows):
            for pair in range(self.pairs):
                for half, (rows, pairs, target) in enumerate(steps):
                    source = (row * self.pairs + pair) * 2 + half
                    links.append((source, ((row ^ rows) * self.pairs + (pair ^ pairs)) * 2 + target))
        return lax.ppermute(value, ("row", "col"), links)

    def rounds(self):
        steps, known = [], 1
        while known < self.rows:
            steps.append(known)
            known = 4 * known
        return steps if known == self.rows and self.pairs == 2 else None


def component_rows(half):
    blobs = 2 * half
    full, step = blobs // 16 * 16, round_up(blobs, 16)
    if blobs - full > 8:
        full = step
    return blobs, full, step, round_up(2 * step + full, 128)


def body_message(first, second):
    columns, half = first.shape[0], first.shape[1] // 3
    blobs, full, step, width = component_rows(half)
    runs = []
    for a in range(3):
        part = slice(a * half, (a + 1) * half)
        runs.append(jnp.concatenate([first[:, part], second[:, part]], axis=1))
    tail = max(blobs - full, 0)
    gap = lambda n: jnp.zeros((columns, n), first.dtype)
    pieces = [runs[0]]
    if tail:
        pieces += [gap(full + 8 - blobs), runs[2][:, full:], gap(step - full - 8 - tail)]
    else:
        pieces += [gap(step - blobs)]
    pieces += [runs[1], gap(step - blobs), runs[2][:, :full], gap(width - 2 * step - min(full, blobs))]
    return jnp.concatenate([p for p in pieces if p.shape[1]], axis=1)


def rpy_products(source, target):
    apart = [s - t for s, t in zip(source, target)]
    dist_sq = apart[0] * apart[0] + apart[1] * apart[1] + apart[2] * apart[2]
    safe_sq = jnp.where(dist_sq > 0.0, dist_sq, 1.0)
    inv = lax.rsqrt(safe_sq)
    inv_sq = inv * inv
    far = dist_sq >= 4.0
    isotropic = jnp.where(far, inv * (0.75 + 0.5 * inv_sq), 1.0 - 0.28125 * (dist_sq * inv))
    anisotropic = inv * jnp.where(far, inv_sq * (0.75 - 1.5 * inv_sq), 0.09375)
    scaled = [anisotropic * d for d in apart]
    product = {}
    for a in range(3):
        for b in range(a, 3):
            value = scaled[a] * apart[b]
            product[a, b] = product[b, a] = value + isotropic if a == b else value
    return product


def lay_lanes(pieces, half):
    pad = pieces[0].shape[1]
    lanes = round_up(3 * half, 128)
    lane = lax.broadcasted_iota(jnp.int32, (1, 128), 1)
    blocks = []
    for first in range(0, lanes, 128):
        block = None
        for a in range(3):
            low, high = a * half - first, (a + 1) * half - first
            if high <= 0 or low >= 128 or pad != 128:
                continue
            moved = pltpu.roll(pieces[a], low % 128, 1) if low % 128 else pieces[a]
            block = moved if block is None else jnp.where(lane >= low, moved, block)
        blocks.append(block)
    return blocks


def fill_tile(half, body, own_body, pos_ref, store):
    blobs, full, step, width = component_rows(half)
    pad = round_up(half, 128)
    rows = [
        jnp.concatenate([pos_ref[c, pl.ds(2 * body + h, 1), :] for h in range(2)], axis=1)
        for c in range(3)
    ]
    source_rows = jnp.concatenate(rows + [jnp.zeros((5, blobs), jnp.float32)], axis=0)
    columns = round_up(step, 128)
    source_cols = jnp.pad(source_rows, ((0, 0), (0, columns - blobs))).T
    targets = [
        [
            jnp.pad(pos_ref[c, pl.ds(2 * own_body + h, 1), :], ((0, 0), (0, pad - half)))
            for c in range(3)
        ]
        for h in range(2)
    ]
    for first in range(0, blobs, 16):
        source = [source_cols[first : first + 16, c : c + 1] for c in range(3)]
        for h in range(2):
            product = rpy_products(source, targets[h])
            laid = [lay_lanes([product[a, b] for a in range(3)], half) for b in range(3)]
            for at in range(len(laid[0])):
                block = [laid[b][at] for b in range(3)]
                if first < full:
                    for b in range(3):
                        store(b * step + first, h, at, block[b])
                else:
                    mixed = jnp.concatenate([block[0][:8], block[2][:8]], axis=0)
                    store(first, h, at, mixed)
                    store(step + first, h, at, block[1])
    used = 2 * step + full
    for first in range(used, width, 16):
        for h in range(2):
            for at in range(round_up(3 * half, 128) // 128):
                store(first, h, at, jnp.zeros((16, 128), jnp.float32))


def tile_store(out_ref, half, at):
    lanes = round_up(3 * half, 128)

    def store(row, h, block, value):
        lane = h * lanes + block * 128
        out_ref[at, row : row + 16, lane : lane + 128] = value.astype(jnp.bfloat16)

    return store


def tiles_kernel(half, grid, offsets, pos_ref, _, out_ref):
    row, col = lax.axis_index("row"), lax.axis_index("col")
    own_body = row * grid.pairs + col // 2
    for at, offset in enumerate(offsets):
        rows, pairs = [jnp.where(col % 2 == 0, offset[0][i], offset[1][i]) for i in range(2)]
        body = (row ^ rows) * grid.pairs + ((col // 2) ^ pairs)
        fill_tile(half, body, own_body, pos_ref, tile_store(out_ref, half, at))


def listed_tiles_kernel(half, ids_ref, pos_ref, out_ref):
    body = ids_ref[pl.program_id(0) + 1]
    fill_tile(half, body, ids_ref[0], pos_ref, tile_store(out_ref, half, 0))


def make_tiles(grid, offsets, pos, half, after, cost):
    shape = (component_rows(half)[-1], 2 * round_up(3 * half, 128))
    return pl.pallas_call(
        functools.partial(tiles_kernel, half, grid, offsets),
        out_shape=pltpu.VMEM((len(offsets),) + shape, jnp.bfloat16),
        in_specs=[IN_VMEM] * 2,
        out_specs=IN_VMEM,
        cost_estimate=work(cost),
        compiler_params=KERNEL_PARAMS,
    )(in_vmem(pos), in_vmem(after))


def make_listed_tiles(grid, offsets, pos, half):
    row, col = lax.axis_index("row"), lax.axis_index("col")
    rows, pairs = [
        jnp.where(col % 2 == 0, *[jnp.array([o[h][i] for o in offsets], jnp.int32) for h in range(2)])
        for i in range(2)
    ]
    bodies = (row ^ rows) * grid.pairs + ((col // 2) ^ pairs)
    own_body = row * grid.pairs + col // 2
    shape = (component_rows(half)[-1], 2 * round_up(3 * half, 128))
    return pl.pallas_call(
        functools.partial(listed_tiles_kernel, half),
        out_shape=jax.ShapeDtypeStruct((len(offsets),) + shape, jnp.bfloat16),
        grid=(len(offsets),),
        in_specs=[pl.BlockSpec(memory_space=pltpu.SMEM), IN_VMEM],
        out_specs=pl.BlockSpec((1,) + shape, lambda s: (s, 0, 0)),
        cost_estimate=work(0.6 * len(offsets)),
        compiler_params=KERNEL_PARAMS,
    )(jnp.concatenate([own_body[None], bodies]), pos)


def split(value):
    shifted = value * 65537.0
    high = shifted - (shifted - value)
    return high.astype(jnp.bfloat16), (value - high).astype(jnp.bfloat16)


def split_dot(left, right):
    (left_high, left_low), (high, low) = left, right
    count = left_high.shape[0]
    both = jnp.dot(jnp.concatenate([left_high, left_low], axis=0), high, preferred_element_type=jnp.float32)
    return both[:count] + both[count:] + jnp.dot(left_high, low, preferred_element_type=jnp.float32)


def body_product(first, second, high_ref, low_ref):
    narrow, pad = first.shape[1], high_ref.shape[0] // 2
    total = None
    for h, value in enumerate((first, second)):
        used = slice(h * pad, h * pad + narrow)
        term = split_dot(split(value), (high_ref[used, :], low_ref[used, :]))
        total = term if total is None else total + term
    return total


def force_kernel(own_ref, other_ref, high_ref, low_ref, rows_ref, force_ref, message_ref):
    half_index = lax.axis_index("col") % 2
    own, other = own_ref[...], other_ref[...]
    narrow, pad = own.shape[1], high_ref.shape[0] // 2
    force = other_force = None
    for h, value in enumerate((jnp.where(half_index == 0, own, other), jnp.where(half_index == 0, other, own))):
        left = split(jnp.pad(value, ((0, 0), (0, pad - narrow))))
        used = slice(h * pad, (h + 1) * pad)
        term = split_dot(left, (high_ref[used, :], low_ref[used, :]))
        force = term if force is None else force + term
        rows = jnp.pad(rows_ref[h * narrow : (h + 1) * narrow, 0, :], ((0, pad - narrow), (0, 0)))
        term = split_dot(left, split(rows))
        other_force = term if other_force is None else other_force + term
    force_ref[...] = force
    first = jnp.where(half_index == 0, force, other_force)
    second = jnp.where(half_index == 0, other_force, force)
    message_ref[0] = body_message(first, second).astype(jnp.bfloat16)


def first_forces(own, other, high, low, other_inverse):
    columns, narrow = own.shape
    width = component_rows(narrow // 3)[-1]
    values = (own, other, high, low, other_inverse)
    return pl.pallas_call(
        force_kernel,
        out_shape=(
            pltpu.VMEM((columns, narrow), jnp.float32),
            pltpu.VMEM((1, columns, width), jnp.bfloat16),
        ),
        in_specs=[IN_VMEM] * len(values),
        out_specs=(IN_VMEM,) * 2,
        cost_estimate=work(0.7),
        compiler_params=KERNEL_PARAMS,
    )(*[in_vmem(v) for v in values])


def correct_kernel(own_ref, other_ref, part_ref, other_part_ref, force_ref, high_ref, low_ref, updated_ref, residual_ref):
    half_index = lax.axis_index("col") % 2
    own, other = own_ref[...], other_ref[...]
    narrow, lanes = own.shape[1], part_ref.shape[1] // 2
    velocity = part_ref[...] + other_part_ref[...]
    first = jnp.where(half_index == 0, own, other) - velocity[:, :narrow]
    second = jnp.where(half_index == 0, other, own) - velocity[:, lanes : lanes + narrow]
    residual_ref[0] = jnp.where(half_index == 0, first, second)
    updated_ref[0] = force_ref[...] + body_product(first, second, high_ref, low_ref)


def corrected(own, other, part, other_part, force, high, low):
    columns, narrow = own.shape
    out = jax.ShapeDtypeStruct((1, columns, narrow), jnp.float32)
    return pl.pallas_call(
        correct_kernel,
        out_shape=(out, out),
        in_specs=[IN_VMEM] * 7,
        out_specs=(IN_VMEM,) * 2,
        cost_estimate=work(0.8),
        compiler_params=KERNEL_PARAMS,
    )(*[in_vmem(v) for v in (own, other, part, other_part, force, high, low)])


def stage_kernel(inverse_hbm, pos_hbm, slip_hbm, high_ref, low_ref, pos_ref, slip_ref, rows_ref, sems):
    narrow, pad = slip_hbm.shape[1], high_ref.shape[0] // 2
    halves = [pl.ds(h * narrow, narrow) for h in range(2)]
    copies = [pltpu.make_async_copy(inverse_hbm.at[r], rows_ref.at[r], sems.at[h]) for h, r in enumerate(halves)]
    copies.append(pltpu.make_async_copy(pos_hbm, pos_ref, sems.at[2]))
    copies.append(pltpu.make_async_copy(slip_hbm, slip_ref, sems.at[3]))
    for copy in copies:
        copy.start()
    for h in range(2):
        copies[h].wait()
        rows = jnp.pad(rows_ref[h * narrow : (h + 1) * narrow, 0, :], ((0, pad - narrow), (0, 0)))
        high_ref[h * pad : (h + 1) * pad, :], low_ref[h * pad : (h + 1) * pad, :] = split(rows)
    copies[2].wait()
    copies[3].wait()


def staged(inverse, pos, slip):
    narrow = slip.shape[1]
    parts = pltpu.VMEM((2 * round_up(narrow, 128), narrow), jnp.bfloat16)
    values = (inverse, pos, slip)
    return pl.pallas_call(
        stage_kernel,
        out_shape=(parts, parts) + tuple(pltpu.VMEM(v.shape, v.dtype) for v in values[1:]),
        in_specs=[pl.BlockSpec(memory_space=pltpu.HBM)] * 3,
        out_specs=(IN_VMEM,) * 4,
        scratch_shapes=[pltpu.VMEM(inverse.shape, jnp.float32), pltpu.SemaphoreType.DMA((4,))],
        cost_estimate=work(1.1),
        compiler_params=KERNEL_PARAMS,
    )(*[pltpu.with_memory_space_constraint(v, pltpu.HBM) for v in values])


def apply_kernel(count, *refs):
    tiles, message_ref, start, out_ref = refs[:count], refs[count], refs[count + 1 : -1], refs[-1]
    total = start[0][...] if start else None
    for at, tile_ref in enumerate(tiles):
        term = jnp.dot(message_ref[at], tile_ref[0], preferred_element_type=jnp.float32)
        total = term if total is None else total + term
    out_ref[...] = total


def apply_tiles(tiles, message, cost, *start):
    values = [*tiles, message, *start]
    return pl.pallas_call(
        functools.partial(apply_kernel, len(tiles)),
        out_shape=pltpu.VMEM((message.shape[1], tiles[0].shape[2]), jnp.float32),
        in_specs=[IN_VMEM] * len(values),
        out_specs=IN_VMEM,
        cost_estimate=work(cost),
        compiler_params=KERNEL_PARAMS,
    )(*[in_vmem(v) for v in values])


def joined_kernel(stack_ref, near_ref, far_ref, *refs):
    half_index = lax.axis_index("col") % 2
    count, out_ref = stack_ref.shape[0], refs[-1]
    out_ref[:count] = jnp.where(half_index == 0, stack_ref[...], near_ref[...])
    out_ref[count:] = far_ref[...]


def joined(stack, near, far, *before):
    values = (stack, near, far) + before
    return pl.pallas_call(
        joined_kernel,
        out_shape=pltpu.VMEM((2 * stack.shape[0],) + stack.shape[1:], stack.dtype),
        in_specs=[IN_VMEM] * len(values),
        out_specs=IN_VMEM,
        cost_estimate=work(0.05),
        compiler_params=KERNEL_PARAMS,
    )(*[in_vmem(v) for v in values])


def gathered(grid, message, half_index, tiles_of):
    steps = grid.rounds()
    if steps is None:
        both = lax.all_gather(message[0], ("row", "col")).reshape(grid.rows, grid.pairs, 2, *message.shape[1:])
        own = lax.axis_index("row"), lax.axis_index("col") // 2
        offsets = [(r, p) for r in range(grid.rows) for p in range(grid.pairs)]
        ordered = jnp.stack([both[own[0] ^ r, own[1] ^ p, 0] for r, p in offsets])
        weight = jnp.where(half_index == 0, 1, 0).astype(message.dtype)
        return [(ordered * weight, tiles_of([(o, o) for o in offsets], message, TILE_TIME))]
    stack, known = message, [0]
    mine, offsets, tiles = message * jnp.where(half_index == 0, 1, 0).astype(message.dtype), [(0, 0)], None
    for at, step in enumerate(steps):
        near = grid.moved(stack, ((step, 0, 1), (0, 0, 0)))
        far = grid.moved(stack, ((3 * step, 0, 1), (2 * step, 0, 0)))
        offsets = [(k, k ^ step) for k in known] + [(k ^ (2 * step), k ^ (3 * step)) for k in known]
        if at + 1 < len(steps):
            mine = joined(stack, near, far)
            others = swapped(mine)
            stack = jnp.concatenate(
                [jnp.where(half_index == 0, mine, others), jnp.where(half_index == 0, others, mine)], axis=0
            )
            known = [o[0] for o in offsets] + [o[1] for o in offsets]
        else:
            tiles = tiles_of([((low, 0), (high, 0)) for low, high in offsets], near, TILE_TIME)
            mine = joined(stack, near, far, *(tiles if isinstance(tiles, list) else []))
    if tiles is None:
        tiles = tiles_of([((low, 0), (high, 0)) for low, high in offsets], message, TILE_TIME)
    across = grid.moved(mine, ((0, 1, 1), (0, 1, 0)))
    return [
        (mine, tiles),
        (across, tiles_of([((high, 1), (low, 1)) for low, high in offsets], mine, LITTLE)),
    ]


def local(slip, inverse, positions):
    grid = Grid(lax.axis_size("row"), lax.axis_size("col"))
    half_index = lax.axis_index("col") % 2
    own_slip = slip[0]
    columns, narrow = own_slip.shape
    half = narrow // 3
    lanes = 2 * round_up(narrow, 128)
    stay = 2 * component_rows(half)[-1] * lanes * grid.rows * grid.pairs <= VMEM_TILE_BYTES

    other_slip = swapped(own_slip)
    other_inverse = swapped(inverse)
    rows = [jnp.swapaxes(v, 0, 1) for v in (inverse, other_inverse, positions)]
    high, low, pos, own_slip = staged(rows[0], rows[2], own_slip)
    force, message = first_forces(own_slip, other_slip, high, low, rows[1])

    def tiles_of(offsets, after, cost):
        if stay:
            return [make_tiles(grid, [o], pos, half, after, cost) for o in offsets]
        return make_listed_tiles(grid, offsets, pos, half)

    part = []
    for values, tiles in gathered(grid, message, half_index, tiles_of):
        if stay:
            part = [apply_tiles(tiles, values, 0.3 if part else LITTLE, *part)]
        else:
            flat = jnp.swapaxes(values, 0, 1).reshape(columns, -1)
            term = jnp.dot(flat, tiles.reshape(-1, lanes), preferred_element_type=jnp.float32)
            part = [term + part[0]] if part else [term]
    part = part[0]
    return corrected(own_slip, other_slip, part, swapped(part), force, high, low)


def solution(mesh):
    in_specs = (
        P(("groups", "row", "col"), None, None),
        P(("groups", "row", "col"), None, None),
        P("groups", None, None),
    )
    out_specs = (P(("groups", "row", "col"), None, None), P(("groups", "row", "col"), None, None))
    return jax.shard_map(local, mesh=mesh, in_specs=in_specs, out_specs=out_specs, check_vma=False)
```

```python
import functools

import jax
import jax.numpy as jnp
from jax import lax
from jax.experimental import pallas as pl
from jax.experimental.pallas import tpu as pltpu
from jax.sharding import PartitionSpec as P

VMEM_TILE_BYTES = 16 * 2**20
TILE_TIME, EARLY_COST, LITTLE = 0.6, 0.3, 0.01
EARLY = 2
IN_VMEM = pl.BlockSpec(memory_space=pltpu.VMEM)
KERNEL_PARAMS = pltpu.CompilerParams(vmem_limit_bytes=48 * 2**20)


def work(microseconds):
    return pl.CostEstimate(flops=int(microseconds * 1.15e9), bytes_accessed=0, transcendentals=0)


def in_vmem(value):
    return pltpu.with_memory_space_constraint(value, pltpu.VMEM)


def round_up(value, step):
    return (value + step - 1) // step * step


def swapped(value):
    pairs = [(source, source ^ 1) for source in range(lax.axis_size("col"))]
    return lax.ppermute(value, "col", pairs)


class Grid:
    def __init__(self, row_count, col_count):
        self.rows, self.pairs = row_count, col_count // 2
        self.steps, known = [], 1
        while known < self.rows:
            self.steps.append(known)
            known = 4 * known
        self.fits = known == self.rows and self.pairs == 2

    def turned(self, row, turns):
        for step, turn in zip(self.steps, turns):
            digit = row // step % 4
            row = row + ((digit + turn) % 4 - digit) * step
        return row

    def moved(self, value, moves):
        links = []
        for row in range(self.rows):
            for pair in range(self.pairs):
                for half, (turns, other, target) in enumerate(moves):
                    source = (row * self.pairs + pair) * 2 + half
                    links.append((source, (self.turned(row, turns) * self.pairs + (pair ^ other)) * 2 + target))
        return lax.ppermute(value, ("row", "col"), links)

    def digit(self, at, turn):
        return tuple(turn if i == at else 0 for i in range(len(self.steps)))


def component_rows(half):
    blobs = 2 * half
    full, step = blobs // 16 * 16, round_up(blobs, 16)
    if blobs - full > 8:
        full = step
    return blobs, full, step, round_up(2 * step + full, 128)


def body_message(first, second):
    columns, half = first.shape[0], first.shape[1] // 3
    blobs, full, step, width = component_rows(half)
    runs = []
    for a in range(3):
        part = slice(a * half, (a + 1) * half)
        runs.append(jnp.concatenate([first[:, part], second[:, part]], axis=1))
    tail = max(blobs - full, 0)
    gap = lambda n: jnp.zeros((columns, n), first.dtype)
    pieces = [runs[0]]
    if tail:
        pieces += [gap(full + 8 - blobs), runs[2][:, full:], gap(step - full - 8 - tail)]
    else:
        pieces += [gap(step - blobs)]
    pieces += [runs[1], gap(step - blobs), runs[2][:, :full], gap(width - 2 * step - min(full, blobs))]
    return jnp.concatenate([p for p in pieces if p.shape[1]], axis=1)


def rpy_products(source, target):
    apart = [s - t for s, t in zip(source, target)]
    dist_sq = apart[0] * apart[0] + apart[1] * apart[1] + apart[2] * apart[2]
    safe_sq = jnp.where(dist_sq > 0.0, dist_sq, 1.0)
    inv = lax.rsqrt(safe_sq)
    inv_sq = inv * inv
    far = dist_sq >= 4.0
    isotropic = jnp.where(far, inv * (0.75 + 0.5 * inv_sq), 1.0 - 0.28125 * (dist_sq * inv))
    anisotropic = inv * jnp.where(far, inv_sq * (0.75 - 1.5 * inv_sq), 0.09375)
    scaled = [anisotropic * d for d in apart]
    product = {}
    for a in range(3):
        for b in range(a, 3):
            value = scaled[a] * apart[b]
            product[a, b] = product[b, a] = value + isotropic if a == b else value
    return product


def lay_lanes(pieces, half):
    pad = pieces[0].shape[1]
    lanes = round_up(3 * half, 128)
    lane = lax.broadcasted_iota(jnp.int32, (1, 128), 1)
    blocks = []
    for first in range(0, lanes, 128):
        block = None
        for a in range(3):
            low, high = a * half - first, (a + 1) * half - first
            if high <= 0 or low >= 128 or pad != 128:
                continue
            moved = pltpu.roll(pieces[a], low % 128, 1) if low % 128 else pieces[a]
            block = moved if block is None else jnp.where(lane >= low, moved, block)
        blocks.append(block)
    return blocks


def fill_tile(half, body, own_body, pos_ref, store):
    blobs, full, step, width = component_rows(half)
    pad = round_up(half, 128)
    rows = [
        jnp.concatenate([pos_ref[c, pl.ds(2 * body + h, 1), :] for h in range(2)], axis=1)
        for c in range(3)
    ]
    source_rows = jnp.concatenate(rows + [jnp.zeros((5, blobs), jnp.float32)], axis=0)
    columns = round_up(step, 128)
    source_cols = jnp.pad(source_rows, ((0, 0), (0, columns - blobs))).T
    targets = [
        [
            jnp.pad(pos_ref[c, pl.ds(2 * own_body + h, 1), :], ((0, 0), (0, pad - half)))
            for c in range(3)
        ]
        for h in range(2)
    ]
    for first in range(0, blobs, 16):
        source = [source_cols[first : first + 16, c : c + 1] for c in range(3)]
        for h in range(2):
            product = rpy_products(source, targets[h])
            laid = [lay_lanes([product[a, b] for a in range(3)], half) for b in range(3)]
            for at in range(len(laid[0])):
                block = [laid[b][at] for b in range(3)]
                if first < full:
                    for b in range(3):
                        store(b * step + first, h, at, block[b])
                else:
                    mixed = jnp.concatenate([block[0][:8], block[2][:8]], axis=0)
                    store(first, h, at, mixed)
                    store(step + first, h, at, block[1])
    used = 2 * step + full
    for first in range(used, width, 16):
        for h in range(2):
            for at in range(round_up(3 * half, 128) // 128):
                store(first, h, at, jnp.zeros((16, 128), jnp.float32))


def tile_store(out_ref, half, at):
    lanes = round_up(3 * half, 128)

    def store(row, h, block, value):
        lane = h * lanes + block * 128
        out_ref[at, row : row + 16, lane : lane + 128] = value.astype(jnp.bfloat16)

    return store


def tiles_kernel(half, grid, offsets, pos_ref, _, out_ref):
    row, col = lax.axis_index("row"), lax.axis_index("col")
    own_body = row * grid.pairs + col // 2
    for at, offset in enumerate(offsets):
        bodies = [grid.turned(row, turns) * grid.pairs + ((col // 2) ^ other) for turns, other in offset]
        body = jnp.where(col % 2 == 0, *bodies)
        fill_tile(half, body, own_body, pos_ref, tile_store(out_ref, half, at))


def listed_tiles_kernel(half, ids_ref, pos_ref, out_ref):
    body = ids_ref[pl.program_id(0) + 1]
    fill_tile(half, body, ids_ref[0], pos_ref, tile_store(out_ref, half, 0))


def make_tiles(grid, offsets, pos, half, after, cost):
    shape = (component_rows(half)[-1], 2 * round_up(3 * half, 128))
    return pl.pallas_call(
        functools.partial(tiles_kernel, half, grid, offsets),
        out_shape=pltpu.VMEM((len(offsets),) + shape, jnp.bfloat16),
        in_specs=[IN_VMEM] * 2,
        out_specs=IN_VMEM,
        cost_estimate=work(cost),
        compiler_params=KERNEL_PARAMS,
    )(in_vmem(pos), in_vmem(after))


def make_listed_tiles(grid, offsets, pos, half):
    row, col = lax.axis_index("row"), lax.axis_index("col")
    own_body = row * grid.pairs + col // 2
    bodies = [
        jnp.where(col % 2 == 0, *[grid.turned(row, t) * grid.pairs + ((col // 2) ^ other) for t, other in offset])
        for offset in offsets
    ]
    shape = (component_rows(half)[-1], 2 * round_up(3 * half, 128))
    return pl.pallas_call(
        functools.partial(listed_tiles_kernel, half),
        out_shape=jax.ShapeDtypeStruct((len(offsets),) + shape, jnp.bfloat16),
        grid=(len(offsets),),
        in_specs=[pl.BlockSpec(memory_space=pltpu.SMEM), IN_VMEM],
        out_specs=pl.BlockSpec((1,) + shape, lambda s: (s, 0, 0)),
        cost_estimate=work(0.6 * len(offsets)),
        compiler_params=KERNEL_PARAMS,
    )(jnp.stack([own_body] + bodies).astype(jnp.int32), pos)


def split(value):
    shifted = value * 65537.0
    high = shifted - (shifted - value)
    return high.astype(jnp.bfloat16), (value - high).astype(jnp.bfloat16)


def split_dot(left, right):
    (left_high, left_low), (high, low) = left, right
    count = left_high.shape[0]
    both = jnp.dot(jnp.concatenate([left_high, left_low], axis=0), high, preferred_element_type=jnp.float32)
    return both[:count] + both[count:] + jnp.dot(left_high, low, preferred_element_type=jnp.float32)


def body_product(first, second, high_ref, low_ref):
    narrow, pad = first.shape[1], high_ref.shape[0] // 2
    total = None
    for h, value in enumerate((first, second)):
        used = slice(h * pad, h * pad + narrow)
        term = split_dot(split(value), (high_ref[used, :], low_ref[used, :]))
        total = term if total is None else total + term
    return total


def force_kernel(own_ref, other_ref, high_ref, low_ref, rows_ref, force_ref, message_ref):
    half_index = lax.axis_index("col") % 2
    own, other = own_ref[...], other_ref[...]
    narrow, pad = own.shape[1], high_ref.shape[0] // 2
    force = other_force = None
    for h, value in enumerate((jnp.where(half_index == 0, own, other), jnp.where(half_index == 0, other, own))):
        left = split(jnp.pad(value, ((0, 0), (0, pad - narrow))))
        used = slice(h * pad, (h + 1) * pad)
        term = split_dot(left, (high_ref[used, :], low_ref[used, :]))
        force = term if force is None else force + term
        rows = jnp.pad(rows_ref[h * narrow : (h + 1) * narrow, 0, :], ((0, pad - narrow), (0, 0)))
        term = split_dot(left, split(rows))
        other_force = term if other_force is None else other_force + term
    force_ref[...] = force
    first = jnp.where(half_index == 0, force, other_force)
    second = jnp.where(half_index == 0, other_force, force)
    message_ref[0] = body_message(first, second).astype(jnp.bfloat16)


def first_forces(own, other, high, low, other_inverse):
    columns, narrow = own.shape
    width = component_rows(narrow // 3)[-1]
    values = (own, other, high, low, other_inverse)
    return pl.pallas_call(
        force_kernel,
        out_shape=(
            pltpu.VMEM((columns, narrow), jnp.float32),
            pltpu.VMEM((1, columns, width), jnp.bfloat16),
        ),
        in_specs=[IN_VMEM] * len(values),
        out_specs=(IN_VMEM,) * 2,
        cost_estimate=work(0.7),
        compiler_params=KERNEL_PARAMS,
    )(*[in_vmem(v) for v in values])


def correct_kernel(own_ref, other_ref, part_ref, other_part_ref, force_ref, high_ref, low_ref, updated_ref, residual_ref):
    half_index = lax.axis_index("col") % 2
    own, other = own_ref[...], other_ref[...]
    narrow, lanes = own.shape[1], part_ref.shape[1] // 2
    velocity = part_ref[...] + other_part_ref[...]
    first = jnp.where(half_index == 0, own, other) - velocity[:, :narrow]
    second = jnp.where(half_index == 0, other, own) - velocity[:, lanes : lanes + narrow]
    residual_ref[0] = jnp.where(half_index == 0, first, second)
    updated_ref[0] = force_ref[...] + body_product(first, second, high_ref, low_ref)


def corrected(own, other, part, other_part, force, high, low):
    columns, narrow = own.shape
    out = jax.ShapeDtypeStruct((1, columns, narrow), jnp.float32)
    return pl.pallas_call(
        correct_kernel,
        out_shape=(out, out),
        in_specs=[IN_VMEM] * 7,
        out_specs=(IN_VMEM,) * 2,
        cost_estimate=work(0.8),
        compiler_params=KERNEL_PARAMS,
    )(*[in_vmem(v) for v in (own, other, part, other_part, force, high, low)])


def stage_kernel(inverse_hbm, pos_hbm, slip_hbm, high_ref, low_ref, pos_ref, slip_ref, rows_ref, sems):
    narrow, pad = slip_hbm.shape[1], high_ref.shape[0] // 2
    halves = [pl.ds(h * narrow, narrow) for h in range(2)]
    copies = [pltpu.make_async_copy(inverse_hbm.at[r], rows_ref.at[r], sems.at[h]) for h, r in enumerate(halves)]
    copies.append(pltpu.make_async_copy(pos_hbm, pos_ref, sems.at[2]))
    copies.append(pltpu.make_async_copy(slip_hbm, slip_ref, sems.at[3]))
    for copy in copies:
        copy.start()
    for h in range(2):
        copies[h].wait()
        rows = jnp.pad(rows_ref[h * narrow : (h + 1) * narrow, 0, :], ((0, pad - narrow), (0, 0)))
        high_ref[h * pad : (h + 1) * pad, :], low_ref[h * pad : (h + 1) * pad, :] = split(rows)
    copies[2].wait()
    copies[3].wait()


def staged(inverse, pos, slip):
    narrow = slip.shape[1]
    parts = pltpu.VMEM((2 * round_up(narrow, 128), narrow), jnp.bfloat16)
    values = (inverse, pos, slip)
    return pl.pallas_call(
        stage_kernel,
        out_shape=(parts, parts) + tuple(pltpu.VMEM(v.shape, v.dtype) for v in values[1:]),
        in_specs=[pl.BlockSpec(memory_space=pltpu.HBM)] * 3,
        out_specs=(IN_VMEM,) * 4,
        scratch_shapes=[pltpu.VMEM(inverse.shape, jnp.float32), pltpu.SemaphoreType.DMA((4,))],
        cost_estimate=work(1.1),
        compiler_params=KERNEL_PARAMS,
    )(*[pltpu.with_memory_space_constraint(v, pltpu.HBM) for v in values])


def apply_kernel(count, *refs):
    tiles, message_ref, start, out_ref = refs[:count], refs[count], refs[count + 1 : -1], refs[-1]
    total = start[0][...] if start else None
    for at, tile_ref in enumerate(tiles):
        term = jnp.dot(message_ref[at], tile_ref[0], preferred_element_type=jnp.float32)
        total = term if total is None else total + term
    out_ref[...] = total


def apply_tiles(tiles, message, cost, *start):
    values = [*tiles, message, *start]
    return pl.pallas_call(
        functools.partial(apply_kernel, len(tiles)),
        out_shape=pltpu.VMEM((message.shape[1], tiles[0].shape[2]), jnp.float32),
        in_specs=[IN_VMEM] * len(values),
        out_specs=IN_VMEM,
        cost_estimate=work(cost),
        compiler_params=KERNEL_PARAMS,
    )(*[in_vmem(v) for v in values])


def joined_kernel(stack_ref, near_ref, far_ref, *refs):
    half_index = lax.axis_index("col") % 2
    count, out_ref = stack_ref.shape[0], refs[-1]
    out_ref[:count] = jnp.where(half_index == 0, near_ref[...], stack_ref[...])
    out_ref[count:] = far_ref[...]


def joined(stack, near, far, *before):
    values = (stack, near, far) + before
    return pl.pallas_call(
        joined_kernel,
        out_shape=pltpu.VMEM((2 * stack.shape[0],) + stack.shape[1:], stack.dtype),
        in_specs=[IN_VMEM] * len(values),
        out_specs=IN_VMEM,
        cost_estimate=work(0.05),
        compiler_params=KERNEL_PARAMS,
    )(*[in_vmem(v) for v in values])


def gathered(grid, message, half_index, tiles_of):
    if not grid.fits:
        both = lax.all_gather(message[0], ("row", "col")).reshape(grid.rows * grid.pairs, 2, *message.shape[1:])
        weight = jnp.where(half_index == 0, 1, 0).astype(message.dtype)
        return [(both[:, 0] * weight, tiles_of(None, message, TILE_TIME))]
    turn = lambda known, at, by: [k[:at] + (by,) + k[at + 1 :] for k in known]
    nil = grid.digit(0, 0)
    stack, known = message, [nil]
    mine, held = message * jnp.where(half_index == 0, 1, 0).astype(message.dtype), [(nil, nil)]
    for at in range(len(grid.steps)):
        near = grid.moved(stack, ((nil, 0, 1), (grid.digit(at, 1), 0, 0)))
        far = grid.moved(stack, ((grid.digit(at, 2), 0, 0), (grid.digit(at, 3), 0, 1)))
        held = [*zip(turn(known, at, 3), known), *zip(turn(known, at, 2), turn(known, at, 1))]
        if at + 1 < len(grid.steps):
            mine = joined(stack, near, far)
            others = swapped(mine)
            stack = jnp.concatenate(
                [jnp.where(half_index == 0, mine, others), jnp.where(half_index == 0, others, mine)], axis=0
            )
            known = [h[0] for h in held] + [h[1] for h in held]
        else:
            own = [((low, 0), (high, 0)) for low, high in held]
            early = tiles_of(own[:EARLY], message, EARLY_COST)
            mine = joined(stack, near, far, *early)
    across = grid.moved(mine, ((nil, 1, 1), (nil, 1, 0)))
    return [
        (mine, early + tiles_of(own[EARLY:], mine, LITTLE)),
        (across, tiles_of([((high, 1), (low, 1)) for low, high in held], mine, LITTLE)),
    ]


def local(slip, inverse, positions):
    grid = Grid(lax.axis_size("row"), lax.axis_size("col"))
    half_index = lax.axis_index("col") % 2
    own_slip = slip[0]
    columns, narrow = own_slip.shape
    half = narrow // 3
    lanes = 2 * round_up(narrow, 128)
    stay = 2 * component_rows(half)[-1] * lanes * grid.rows * grid.pairs <= VMEM_TILE_BYTES

    other_slip = swapped(own_slip)
    other_inverse = swapped(inverse)
    rows = [jnp.swapaxes(v, 0, 1) for v in (inverse, other_inverse, positions)]
    high, low, pos, own_slip = staged(rows[0], rows[2], own_slip)
    force, message = first_forces(own_slip, other_slip, high, low, rows[1])

    def tiles_of(offsets, after, cost):
        if stay:
            return [make_tiles(grid, [o], pos, half, after, cost) for o in offsets]
        return [make_listed_tiles(grid, offsets, pos, half)] if offsets else []

    part = []
    for values, tiles in gathered(grid, message, half_index, tiles_of):
        if stay:
            part = [apply_tiles(tiles, values, 0.3 if part else LITTLE, *part)]
        else:
            for tile in tiles:
                taken, values = values[: tile.shape[0]], values[tile.shape[0] :]
                flat = jnp.swapaxes(taken, 0, 1).reshape(columns, -1)
                term = jnp.dot(flat, tile.reshape(-1, lanes), preferred_element_type=jnp.float32)
                part = [term + part[0]] if part else [term]
    part = part[0]
    return corrected(own_slip, other_slip, part, swapped(part), force, high, low)


def solution(mesh):
    in_specs = (
        P(("groups", "row", "col"), None, None),
        P(("groups", "row", "col"), None, None),
        P("groups", None, None),
    )
    out_specs = (P(("groups", "row", "col"), None, None), P(("groups", "row", "col"), None, None))
    return jax.shard_map(local, mesh=mesh, in_specs=in_specs, out_specs=out_specs, check_vma=False)
```
